256 devices in a mesh: row: 32 (over z, x), col: 8 (over y, core).
Axes of the slice: x: 4, y: 4, z: 8, core: 2. Of those that a mesh axis runs over, the one named last changes fastest.
Arguments:
- adjoint_source: float32 [2048, 65536], P('col', 'row'), may hold values from -6 to 6
- u_rows: bfloat16 [2, 512, 65536], P(None, None, 'row'), may hold values from -0.25 to 0.25
- diag_inverse: bfloat16 [2, 512, 512], replicated, as said below
- forward_field: bfloat16 [2048, 65536], P('col', 'row'), may hold values from -6 to 6
- panel_coords: bfloat16 [3, 65536], P(None, 'row'), may hold values from -4 to 4
- pair_list: int32 [512, 2], P('row'), may hold values from 0 to 127, as said below
Outputs:
- solved_source: float32 [2048, 65536], P('col', 'row')
- shape_gradient: float32 [512, 3, 512], P('row')
The draws below stay inside these ranges and needn't reach their ends.
Inputs may be any that keep to these rules, and one draw needn't show every extreme that they name: pair_list[p, 0] is a pivot block, 0 or 1; pair_list[p, 1] is a block held by grid row p // 16, i.e. from (p // 16) * 4 to that plus 4 - 1. Each diag_inverse[k] is upper triangular with a positive diagonal.
All inputs are finite; a program needn't handle non-finite values.
Results may differ from the reference program's by a relative error of at most 0.005.
Values may be sent and summed in bfloat16 or wider, within the bound.
No kernel may reach another device: no remote copies, remote signals or barrier semaphores. Data moves between devices by JAX's collectives and lax.ppermute only.
A program may use at most 64 MiB of HBM per device.

```python
import math
import jax
import jax.numpy as jnp
from jax import lax

NB = 512
BLK_DEV = 4
PAIR_DEV = 16
ROWS_DEV = 2048
N = 65536
R = 2048
PAIRS = 512


def draw_diag_inverse(key, part):
    key = jax.random.fold_in(key, 11)
    first, second = jax.random.split(key)
    lines = jnp.arange(NB)[:, None]
    places = jnp.arange(NB)[None, :]
    off = jax.random.normal(first, (2, NB, NB), jnp.float32) * (0.6 / jnp.sqrt(NB * 1.0))
    main = jax.random.uniform(second, (2, NB), jnp.float32, 0.5, 1.5)
    upper = jnp.where(places > lines, off, 0.0)
    whole = jnp.where(places == lines, main[:, :, None], upper)
    return whole.astype(jnp.bfloat16)


def draw_pair_list(key, part):
    key = jax.random.fold_in(key, 5)
    first, second = jax.random.split(key)
    slots = jnp.arange(PAIRS)
    owner = slots // PAIR_DEV
    pivot = jax.random.randint(first, (PAIRS,), 0, 2)
    local = jax.random.randint(second, (PAIRS,), 0, BLK_DEV)
    local = jnp.where(slots == PAIRS - 1, BLK_DEV - 1, local)
    pivot = jnp.where(slots == 0, 0, jnp.where(slots == PAIRS - 1, 1, pivot))
    return jnp.stack([pivot, owner * BLK_DEV + local], axis=1).astype(jnp.int32)


def levels(key, extent, shards, low, high):
    gain, own = 1.0, jax.random.fold_in(key, 6)
    for position, parts in shards:
        steps = jnp.exp(jax.random.uniform(jax.random.fold_in(own, position), (parts,), jnp.float32, low / len(shards), high / len(shards)))
        gain = gain * jnp.repeat(steps, extent[position] // parts).reshape([-1 if axis == position else 1 for axis in range(len(extent))])
    return gain


def normal_values(own_key, shape, deviation, most, cuts=(), held_as=jnp.bfloat16):
    factor_of = levels(own_key, shape, cuts, -0.22, 0.18) if cuts else 1.0
    values = jax.random.normal(own_key, shape, jnp.float32) * deviation * factor_of
    return jnp.minimum(jnp.maximum(values, -most), most).astype(held_as)


def setup_inputs(seed: int = 0) -> dict:
    key_list = jax.random.split(jax.random.key(seed), 7)
    return {
        "adjoint_source": normal_values(key_list[0], (R, N), 1.0, 6.0, ((0, 8), (1, 32)), jnp.float32),
        "u_rows": normal_values(key_list[1], (2, NB, N), NB ** -0.5, 0.25, ((2, 32),)),
        "diag_inverse": draw_diag_inverse(jax.random.fold_in(key_list[6], 71), 0),
        "forward_field": normal_values(key_list[3], (R, N), 1.0, 6.0, ((0, 8), (1, 32))),
        "panel_coords": jnp.clip(jax.random.uniform(key_list[4], (3, N), jnp.float32, -4.0, 4.0) * levels(key_list[4], (3, N), ((1, 32),), -0.4, 0.0), -4.0, 4.0).astype(jnp.bfloat16),
        "pair_list": draw_pair_list(jax.random.fold_in(key_list[6], 71), 0),
    }


def reference(adjoint_source, u_rows, diag_inverse, forward_field, panel_coords, pair_list):
    second = ROWS_DEV
    block_first = adjoint_source[:, 0:NB].astype(jnp.bfloat16)
    solve_first = jnp.dot(block_first, diag_inverse[0], preferred_element_type=jnp.float32).astype(jnp.bfloat16)
    after_first = adjoint_source - jnp.dot(solve_first, u_rows[0], preferred_element_type=jnp.float32)
    block_second = after_first[:, second:second + NB].astype(jnp.bfloat16)
    solve_second = jnp.dot(block_second, diag_inverse[1], preferred_element_type=jnp.float32).astype(jnp.bfloat16)
    updated = after_first - jnp.dot(solve_second, u_rows[1], preferred_element_type=jnp.float32)
    updated = updated.at[:, 0:NB].set(solve_first.astype(jnp.float32))
    solved = updated.at[:, second:second + NB].set(solve_second.astype(jnp.float32))
    solved_rows = solved.astype(jnp.bfloat16)
    lefts = jnp.stack([jnp.concatenate([solve_first, forward_field[:, 0:NB]], axis=0), jnp.concatenate([solve_second, forward_field[:, second:second + NB]], axis=0)])
    pivot_coords = jnp.stack([panel_coords[:, 0:NB], panel_coords[:, second:second + NB]]).astype(jnp.float32)
    scale = 1.0 / math.sqrt(R)

    def one_pair(pair):
        which = pair[0]
        start = (pair[1] * NB).astype(jnp.int32)
        left = lax.dynamic_index_in_dim(lefts, which, 0, keepdims=False)
        right = jnp.concatenate([lax.dynamic_slice_in_dim(forward_field, start, NB, 1), lax.dynamic_slice_in_dim(solved_rows, start, NB, 1)], axis=0)
        influence = jnp.dot(left.T, right, preferred_element_type=jnp.float32) * scale
        source = lax.dynamic_index_in_dim(pivot_coords, which, 0, keepdims=False)
        target = lax.dynamic_slice_in_dim(panel_coords, start, NB, 1).astype(jnp.float32)
        diff = source[:, :, None] - target[:, None, :]
        spread = lax.optimization_barrier(jnp.sum(diff * diff, axis=0)) + 1.0
        kernel = -diff / (spread * jnp.sqrt(spread))
        return lax.optimization_barrier(jnp.sum(influence[None] * kernel, axis=2))
    gradient = lax.map(one_pair, pair_list)
    return (solved, gradient)
```

```python
import functools
import math

import jax
import jax.numpy as jnp
from jax import lax
from jax.experimental import pallas as pl
from jax.experimental.pallas import tpu as pltpu
from jax.sharding import PartitionSpec as P

NZ, NX, NY, NC = 8, 4, 4, 2
ROWS, COLS = NZ * NX, NY * NC
NB, SIDES, WIDTH = 512, 256, 2048
QB = WIDTH // NB
PIECE = SIDES // NX
CROWS = 16
FAR = 3
BF, F32 = jnp.bfloat16, jnp.float32
VMEM_LIMIT = 48 * 1024 * 1024


def node(z, x):
    return (z % NZ) * NX + x % NX


def shift(dz, dx, zs=range(NZ)):
    return [(node(z, x), node(z + dz, x + dx)) for z in zs for x in range(NX)]


def closed(pairs):
    out, back = dict(pairs), {d: s for s, d in pairs}
    for last in back:
        if last not in dict(pairs):
            first = last
            while first in back:
                first = back[first]
            out[last] = first
    return out


def send(value, pairs0, pairs1=None, idle="core"):
    maps = [closed(pairs0), closed(pairs0 if pairs1 is None else pairs1)]
    flip = 3 if idle == "y3" else 1
    out = {}
    for row in range(ROWS):
        free = [row not in maps[0], row not in maps[1]]
        for y in range(NY):
            for core in range(NC):
                me = row * COLS + y * NC + core
                if not free[core]:
                    out[me] = maps[core][row] * COLS + y * NC + core
                elif all(free) and idle == "core":
                    out[me] = row * COLS + y * NC + 1 - core
                else:
                    out[me] = row * COLS + (y ^ flip) * NC + core
    return lax.ppermute(value, ("row", "col"), sorted(out.items()))


def pick(index, values):
    out = values[-1]
    for k in range(len(values) - 2, -1, -1):
        out = jnp.where(index == k, values[k], out)
    return out


def send_x(value, k, idle):
    return send(value, shift(0, k, zs=(0,)), idle=idle)


def spread_z(value, z, core, mode):
    idle = {"plain": "core", "crossed": "y1", "limited": "y3"}[mode]
    crossed = mode == "crossed"
    near_zs = {"plain": (range(NZ),) * 2, "crossed": (range(NZ),) * 2, "limited": ((0, 3, 5), (0, 3))}[mode]

    def both(value, step, zs_plus, zs_minus):
        up, down = shift(step, 0, zs_plus), shift(-step, 0, zs_minus)
        if not crossed:
            return send(value, up, idle=idle), send(value, down, idle=idle)
        a, b = send(value, up, down, idle=idle), send(value, down, up, idle=idle)
        return jnp.where(core == 0, a, b), jnp.where(core == 0, b, a)

    plus, minus = both(value, FAR, (0,), (0,))
    value = jnp.where(z == FAR, plus, jnp.where(z == NZ - FAR, minus, value))
    plus, minus = both(value, 1, *near_zs)
    value = jnp.where((z == 1) | (z == 4) | (z == 6), plus, value)
    return jnp.where((z == 2) | (z == 7), minus, value)


def gather_x(value, twist):
    return [send(value, shift(0, j), shift(0, (j + twist - 1) % 3 + 1)) for j in (1, 2, 3)]


def moved(j, core, twist):
    return j if j == 0 else jnp.where(core == 0, j, (j + twist - 1) % 3 + 1)


def assemble(values, source, x, core, twist):
    held = [(x - moved(j, core, twist) - source) % NX for j in range(NX)]
    parts = []
    for p in range(NX):
        part = values[NX - 1]
        for j in range(NX - 1):
            part = jnp.where(held[j] == p, values[j], part)
        parts.append(part)
    return jnp.concatenate(parts, axis=0)


def dot(a, b):
    return jnp.dot(a, b, preferred_element_type=F32)


def weight_kernel(pivot_ref, target_ref, out_ref):
    source = pivot_ref[0].astype(F32)
    target = target_ref[...].astype(F32)
    source = source.T
    total = None
    for c in range(3):
        d = source[:, c : c + 1] - target[c : c + 1, :]
        total = d * d if total is None else total + d * d
    r = lax.rsqrt(total + 1.0)
    out_ref[0] = r * r * r


def weights(pivots, targets):
    return pl.pallas_call(
        weight_kernel,
        grid=(2, QB),
        in_specs=[
            pl.BlockSpec((1, CROWS, NB), lambda a, q: (a, 0, 0)),
            pl.BlockSpec((CROWS, NB), lambda a, q: (0, q)),
        ],
        out_specs=pl.BlockSpec((1, NB, NB), lambda a, q: (a, 0, q)),
        out_shape=jax.ShapeDtypeStruct((2, NB, WIDTH), F32),
        cost_estimate=pl.CostEstimate(flops=12 * NB * WIDTH * 2, bytes_accessed=8 * NB * WIDTH, transcendentals=2 * NB * WIDTH),
        compiler_params=pltpu.CompilerParams(vmem_limit_bytes=VMEM_LIMIT),
    )(pivots, targets)


def final_kernel(
    info, after_ref, u_ref, field_ref, s0_ref, p0, p1, p2, p3, f0_ref, f1_ref, w_ref, pivot_ref, target_ref,
    solved_ref, grad_ref, s1_ref, left_ref, right_ref, scale_value,
):
    q = pl.program_id(0)
    row = info[0]

    @pl.when(q == 0)
    def _():
        for j, ref in enumerate((p0, p1, p2, p3)):
            s1_ref[pl.ds(pl.multiple_of(info[1 + j] * PIECE, PIECE), PIECE), :] = ref[...]
        left_ref[0, :, 0:SIDES] = s0_ref[...].T
        left_ref[0, :, SIDES:] = f0_ref[...].T
        left_ref[1, :, 0:SIDES] = s1_ref[...].T
        left_ref[1, :, SIDES:] = f1_ref[...].T

    solved_ref[...] = after_ref[...] - dot(s1_ref[...], u_ref[0])

    @pl.when((q == 0) & (row == 0))
    def _():
        solved_ref[...] = s0_ref[...].astype(F32)

    @pl.when((q == 0) & (row == 1))
    def _():
        solved_ref[...] = s1_ref[...].astype(F32)

    right_ref[0:SIDES, :] = field_ref[...]
    right_ref[SIDES:, :] = solved_ref[...].astype(BF)
    target = target_ref[0:8, :]
    lines = lax.broadcasted_iota(jnp.int32, target.shape, 0)
    target = jnp.where(lines == 3, 1.0, target.astype(F32)).astype(BF)
    for a in range(2):
        influence = dot(left_ref[a], right_ref[...])
        weighted = (influence * w_ref[a]).astype(BF)
        sums = lax.dot_general(target, weighted, (((1,), (1,)), ((), ())), preferred_element_type=F32)
        source = pivot_ref[a].astype(F32)
        for c in range(3):
            grad_ref[c, pl.ds(a * QB + q, 1), :] = (
                sums[c : c + 1, :] - source[c : c + 1, :] * sums[3:4, :]
            ) * scale_value


def final(info, after, u_rows, field, s0, parts, f0, f1, w, pivots, targets, scale_value):
    def whole(shape):
        return pl.BlockSpec(shape, lambda q, info: (0,) * len(shape))

    def body(info, *refs):
        final_kernel(info, *refs, scale_value)

    return pl.pallas_call(
        body,
        grid_spec=pltpu.PrefetchScalarGridSpec(
            num_scalar_prefetch=1,
            grid=(QB,),
            in_specs=[
                pl.BlockSpec((SIDES, NB), lambda q, info: (0, q)),
                pl.BlockSpec((1, NB, NB), lambda q, info: (1, 0, q)),
                pl.BlockSpec((SIDES, NB), lambda q, info: (0, q)),
                whole((SIDES, NB)),
                *[whole((PIECE, NB))] * NX,
                whole((SIDES, NB)),
                whole((SIDES, NB)),
                pl.BlockSpec((2, NB, NB), lambda q, info: (0, 0, q)),
                whole((2, CROWS, NB)),
                pl.BlockSpec((CROWS, NB), lambda q, info: (0, q)),
            ],
            out_specs=[
                pl.BlockSpec((SIDES, NB), lambda q, info: (0, q)),
                whole((3, 2 * QB, NB)),
            ],
            scratch_shapes=[
                pltpu.VMEM((SIDES, NB), BF),
                pltpu.VMEM((2, NB, 2 * SIDES), BF),
                pltpu.VMEM((2 * SIDES, NB), BF),
            ],
        ),
        out_shape=[
            jax.ShapeDtypeStruct((SIDES, WIDTH), F32),
            jax.ShapeDtypeStruct((3, 2 * QB, NB), F32),
        ],
        cost_estimate=pl.CostEstimate(
            flops=2 * SIDES * NB * WIDTH + 8 * SIDES * NB * WIDTH, bytes_accessed=16 * 2**20, transcendentals=0
        ),
        compiler_params=pltpu.CompilerParams(vmem_limit_bytes=VMEM_LIMIT),
    )(info, after, u_rows, field, s0, *parts, f0, f1, w, pivots, targets)


def choose_kernel(slots, a_ref, b_ref, c_ref, d_ref, out_ref, sum_ref):
    sum_ref[...] = (a_ref[...] + c_ref[...]) + (b_ref[...] + d_ref[...])
    for p in range(out_ref.shape[0]):
        for c in range(3):
            out_ref[p, pl.ds(c, 1), :] = sum_ref[c, pl.ds(slots[p], 1), :]


def choose(slots, tables):
    shape = (3, 2 * QB, NB)
    whole = pl.BlockSpec(shape, lambda i, slots: (0, 0, 0))
    out = (slots.shape[0], 3, NB)
    return pl.pallas_call(
        choose_kernel,
        grid_spec=pltpu.PrefetchScalarGridSpec(
            num_scalar_prefetch=1,
            grid=(1,),
            in_specs=[whole] * 4,
            out_specs=pl.BlockSpec(out, lambda i, slots: (0, 0, 0)),
            scratch_shapes=[pltpu.VMEM(shape, F32)],
        ),
        out_shape=jax.ShapeDtypeStruct(out, F32),
    )(slots, *tables)


def on_device(adjoint_source, u_rows, diag_inverse, forward_field, panel_coords, pair_list):
    row = lax.axis_index("row")
    z, x = row // NX, row % NX
    core = lax.axis_index("col") % NC
    head = adjoint_source[:, 0:NB]
    own_field = forward_field[:, 0:NB]
    coords = jnp.pad(panel_coords, ((0, CROWS - 3), (0, 0)))

    solve0 = dot(head.astype(BF), diag_inverse[0]).astype(BF)
    at_one = send_x(solve0, 1, "y3")

    pieces = [
        jnp.concatenate([own_field[k * PIECE : (k + 1) * PIECE], coords[:, 0:NB]], axis=0) for k in range(NX)
    ]
    got = [pieces[0]] + [send_x(pieces[k], k, "core") for k in (1, 2, 3)]
    field = jnp.concatenate([pick(x, got), pick((x - 1) % NX, got)], axis=0)
    field = spread_z(field, z, core, "plain")
    high = PIECE + CROWS
    pivots = jnp.stack([field[PIECE:high], field[high + PIECE :]])
    field = jnp.concatenate([field[0:PIECE], field[high : high + PIECE]], axis=0)
    w = weights(pivots, coords)
    fields = [field] + gather_x(field, 1)
    f0 = assemble([v[0:PIECE] for v in fields], 0, x, core, 1)
    f1 = assemble([v[PIECE:] for v in fields], 1, x, core, 1)

    known0 = jnp.where(x == 0, solve0, at_one)
    block1 = (head - dot(known0, u_rows[0, :, 0:NB])).astype(BF)
    solve1 = dot(block1, diag_inverse[1]).astype(BF)
    quarters = [solve1[k * PIECE : (k + 1) * PIECE] for k in range(NX)]
    got = [quarters[0]] + [send_x(quarters[k], k, "y1") for k in (1, 2, 3)]
    part1 = spread_z(pick((x - 1) % NX, got), z, core, "crossed")
    parts1 = [part1] + gather_x(part1, 2)

    quarters = [solve0[k * PIECE : (k + 1) * PIECE] for k in range(NX)]
    got = [quarters[0], at_one[PIECE : 2 * PIECE]] + [send_x(quarters[k], k, "y3") for k in (2, 3)]
    part0 = spread_z(pick(x, got), z, core, "limited")
    parts0 = [part0] + gather_x(part0, 3)
    s0 = assemble(parts0, 0, x, core, 3)
    after = adjoint_source - dot(s0, u_rows[0])

    held = [(x - moved(j, core, 2) - 1) % NX for j in range(NX)]
    info = jnp.stack([row, *held]).astype(jnp.int32)
    scale_value = 1.0 / math.sqrt(SIDES * COLS)
    solved, table = final(info, after, u_rows, forward_field, s0, parts1, f0, f1, w, pivots, coords, scale_value)

    table = table + lax.ppermute(table, "col", [(c, c ^ 1) for c in range(COLS)])
    others = [lax.ppermute(table, "col", [(c, (c + NC * k) % COLS) for c in range(COLS)]) for k in (1, 2, 3)]
    slots = pair_list[:, 0] * QB + pair_list[:, 1] - row * QB
    gradient = choose(slots, [table, others[0], others[1], others[2]])
    return solved, gradient


def solution(mesh):
    return jax.shard_map(
        on_device,
        mesh=mesh,
        in_specs=(P("col", "row"), P(None, None, "row"), P(), P("col", "row"), P(None, "row"), P("row", None)),
        out_specs=(P("col", "row"), P("row", None, None)),
        check_vma=False,
    )
```

```python
import math

import jax
import jax.numpy as jnp
from jax import lax
from jax.experimental import pallas as pl
from jax.experimental.pallas import tpu as pltpu
from jax.sharding import PartitionSpec as P

NZ, NX, NY, NC = 8, 4, 4, 2
ROWS, COLS = NZ * NX, NY * NC
NB, SIDES, WIDTH = 512, 256, 2048
QB = WIDTH // NB
HALF = SIDES // 2
CROWS = 16
FAR = 3
BF, F32 = jnp.bfloat16, jnp.float32
VMEM_LIMIT = 15 * 1024 * 1024


def node(z, x):
    return (z % NZ) * NX + x % NX


def shift(dz, dx, zs=range(NZ)):
    return [(node(z, x), node(z + dz, x + dx)) for z in zs for x in range(NX)]


def closed(pairs):
    out, back = dict(pairs), {d: s for s, d in pairs}
    for last in back:
        if last not in dict(pairs):
            first = last
            while first in back:
                first = back[first]
            out[last] = first
    return out


def send(value, pairs0, pairs1=None, idle="core"):
    maps = [closed(pairs0), closed(pairs0 if pairs1 is None else pairs1)]
    flip = 3 if idle == "y3" else 1
    out = {}
    for row in range(ROWS):
        free = [row not in maps[0], row not in maps[1]]
        for y in range(NY):
            for core in range(NC):
                me = row * COLS + y * NC + core
                if not free[core]:
                    out[me] = maps[core][row] * COLS + y * NC + core
                elif all(free) and idle == "core":
                    out[me] = row * COLS + y * NC + 1 - core
                else:
                    out[me] = row * COLS + (y ^ flip) * NC + core
    return lax.ppermute(value, ("row", "col"), sorted(out.items()))


def choose(condition, a, b):
    return lax.select(condition, a, b)


def swap_x(value, partner, zs=range(NZ)):
    return send(value, [(node(z, x), node(z, partner[x])) for z in zs for x in range(NX)])


def spread_far(value, z):
    plus = send(value, [(node(a, x), node(b, x)) for a, b in ((0, 3), (3, 2), (2, 1), (1, 0)) for x in range(NX)])
    minus = send(value, [(node(a, x), node(b, x)) for a, b in ((0, 5), (5, 6), (6, 7), (7, 0)) for x in range(NX)])
    return choose(z == 3, plus, choose(z == 5, minus, value))


def spread_near(value, z):
    plus, minus = send(value, shift(1, 0)), send(value, shift(-1, 0))
    value = choose((z == 1) | (z == 4) | (z == 6), plus, value)
    return choose((z == 2) | (z == 7), minus, value)


def gather_x(value, twist):
    return [send(value, shift(0, j), shift(0, (j + twist - 1) % 3 + 1)) for j in (1, 2, 3)]


def moved(j, core, twist):
    return j if j == 0 else jnp.where(core == 0, j, (j + twist - 1) % 3 + 1)


def held(x, core, twist):
    return [(x - moved(j, core, twist)) % NX for j in range(NX)]


def dot(a, b):
    return jnp.dot(a, b, preferred_element_type=F32)


def weight_kernel(pivot_ref, target_ref, out_ref):
    source = pivot_ref[0].astype(F32)
    target = target_ref[...].astype(F32)
    source = source.T
    total = None
    for c in range(3):
        d = source[:, c : c + 1] - target[c : c + 1, :]
        total = d * d if total is None else total + d * d
    r = lax.rsqrt(total + 1.0)
    out_ref[0] = (r * r * r).astype(BF)


def weights(pivots, targets):
    return pl.pallas_call(
        weight_kernel,
        grid=(2, QB),
        in_specs=[
            pl.BlockSpec((1, CROWS, NB), lambda a, q: (a, 0, 0)),
            pl.BlockSpec((CROWS, NB), lambda a, q: (0, q)),
        ],
        out_specs=pl.BlockSpec((1, NB, NB), lambda a, q: (a, 0, q)),
        out_shape=jax.ShapeDtypeStruct((2, NB, WIDTH), BF),
        cost_estimate=pl.CostEstimate(
            flops=12 * NB * WIDTH * 2, bytes_accessed=8 * NB * WIDTH, transcendentals=2 * NB * WIDTH
        ),
        compiler_params=pltpu.CompilerParams(vmem_limit_bytes=VMEM_LIMIT),
    )(pivots, targets)


def final_kernel(
    info, source_ref, u_ref, field_ref, p0, p1, p2, p3, own_ref, other_ref, w_ref, pivot_ref, target_ref,
    solved_ref, grad_ref, s_ref, both_ref, left_ref, right_ref, scale_value,
):
    q = pl.program_id(0)
    row = info[0]

    @pl.when(q == 0)
    def _():
        for j, ref in enumerate((p0, p1, p2, p3)):
            column = info[2 + j]
            a = (column ^ (column >> 1)) & 1
            start = pl.multiple_of((column >> 1) * HALF, HALF)
            s_ref[a, pl.ds(start, HALF), :] = ref[...]
        for a in range(2):
            both_ref[:, a * NB : (a + 1) * NB] = s_ref[a]
            left_ref[a, :, 0:SIDES] = s_ref[a].T
        left_ref[info[1], :, SIDES:] = own_ref[...].T
        left_ref[1 - info[1], :, SIDES:] = other_ref[...].T

    solved_ref[...] = source_ref[...] - dot(both_ref[...], u_ref[...])

    @pl.when((q == 0) & (row < 2))
    def _():
        solved_ref[...] = s_ref[row].astype(F32)

    right_ref[0:SIDES, :] = field_ref[...]
    right_ref[SIDES:, :] = solved_ref[...].astype(BF)
    target = target_ref[0:8, :]
    lines = lax.broadcasted_iota(jnp.int32, target.shape, 0)
    target = jnp.where(lines == 3, 1.0, target.astype(F32)).astype(BF)
    for a in range(2):
        influence = dot(left_ref[a], right_ref[...])
        weighted = (influence * w_ref[a].astype(F32)).astype(BF)
        sums = lax.dot_general(target, weighted, (((1,), (1,)), ((), ())), preferred_element_type=F32)
        source = pivot_ref[a].astype(F32)
        for c in range(3):
            grad_ref[c, pl.ds(a * QB + q, 1), :] = (
                sums[c : c + 1, :] - source[c : c + 1, :] * sums[3:4, :]
            ) * scale_value


def final(info, source, u_rows, field, parts, fields, w, pivots, targets, scale_value):
    def whole(shape):
        return pl.BlockSpec(shape, lambda q, info: (0,) * len(shape))

    def body(info, *refs):
        final_kernel(info, *refs, scale_value)

    return pl.pallas_call(
        body,
        grid_spec=pltpu.PrefetchScalarGridSpec(
            num_scalar_prefetch=1,
            grid=(QB,),
            in_specs=[
                pl.BlockSpec((SIDES, NB), lambda q, info: (0, q)),
                pl.BlockSpec((2 * NB, NB), lambda q, info: (0, q)),
                pl.BlockSpec((SIDES, NB), lambda q, info: (0, q)),
                *[whole((HALF, NB))] * NX,
                *[whole((SIDES, NB))] * 2,
                pl.BlockSpec((2, NB, NB), lambda q, info: (0, 0, q)),
                whole((2, CROWS, NB)),
                pl.BlockSpec((CROWS, NB), lambda q, info: (0, q)),
            ],
            out_specs=[
                pl.BlockSpec((SIDES, NB), lambda q, info: (0, q)),
                whole((3, 2 * QB, NB)),
            ],
            scratch_shapes=[
                pltpu.VMEM((2, SIDES, NB), BF),
                pltpu.VMEM((SIDES, 2 * NB), BF),
                pltpu.VMEM((2, NB, 2 * SIDES), BF),
                pltpu.VMEM((2 * SIDES, NB), BF),
            ],
        ),
        out_shape=[
            jax.ShapeDtypeStruct((SIDES, WIDTH), F32),
            jax.ShapeDtypeStruct((3, 2 * QB, NB), F32),
        ],
        cost_estimate=pl.CostEstimate(
            flops=4 * SIDES * NB * WIDTH + 8 * SIDES * NB * WIDTH, bytes_accessed=14 * 2**20, transcendentals=0
        ),
        compiler_params=pltpu.CompilerParams(vmem_limit_bytes=VMEM_LIMIT),
    )(info, source, u_rows.reshape(2 * NB, WIDTH), field, *parts, *fields, w, pivots, targets)


def spread_fields(value, z, x, core):
    along_x = ((0, 3), (1, 2))
    steps0 = [
        [(node(0, a), node(0, b)) for a, b in along_x],
        [(node(a, x), node(b, x)) for a, b in ((0, 3),) for x in range(NX)],
        [(node(a, x), node(b, x)) for a, b in ((0, 6), (3, 5)) for x in range(NX)],
        [(node(a, x), node(b, x)) for a, b in ((0, 1), (3, 2), (6, 7), (5, 4)) for x in range(NX)],
    ]
    steps1 = [
        [(node(a, x), node(b, x)) for a, b in ((0, 5),) for x in (0, 1)],
        [(node(a, x), node(b, x)) for a, b in ((0, 2), (5, 3)) for x in (0, 1)],
        [(node(a, x), node(b, x)) for a, b in ((0, 7), (5, 6), (2, 1), (3, 4)) for x in (0, 1)],
        [(node(z, a), node(z, b)) for a, b in along_x for z in range(NZ)],
    ]
    near = (z == 1) | (z == 4) | (z == 7)
    here0 = [(z == 0) & (x >= 2), z == 3, (z == 6) | (z == 5), near | (z == 2)]
    here1 = [z == 5, (z == 2) | (z == 3), near | (z == 6), x >= 2]
    for k in range(4):
        got = send(value, steps0[k], steps1[k])
        value = jnp.where(jnp.where(core == 0, here0[k], here1[k]), got, value)
        yield value
    yield send(value, [(node(z, x), node(z, x ^ 1)) for z in range(NZ) for x in range(NX)])


def on_device(adjoint_source, u_rows, diag_inverse, forward_field, panel_coords, pair_list):
    row = lax.axis_index("row")
    z, x = row // NX, row % NX
    core = lax.axis_index("col") % NC
    head = adjoint_source[:, 0:NB]
    coords = jnp.pad(panel_coords, ((0, CROWS - 3), (0, 0)))

    solve0 = dot(head.astype(BF), diag_inverse[0]).astype(BF)
    at_one = send(solve0, [(node(0, 0), node(0, 1))])

    own_field, _ = lax.optimization_barrier((forward_field[:, 0:NB], solve0))
    field_steps = list(spread_fields(own_field, z, x, core))

    known0 = choose(x == 0, solve0, at_one)
    block1 = (head - dot(known0, u_rows[0, :, 0:NB])).astype(BF)
    solve1 = dot(block1, diag_inverse[1]).astype(BF)

    mine = choose(x == 0, solve0, solve1)
    own_coords = coords[:, 0:NB]
    first = jnp.concatenate([mine[0:HALF], own_coords], axis=0)
    second = jnp.concatenate([mine[HALF:], own_coords], axis=0)
    solves = choose(x >= 2, swap_x(second, (3, 2, 1, 0), zs=(0,)), first)
    solves = spread_near(spread_far(solves, z), z)
    coords_own = solves[HALF:]
    coords_other = swap_x(coords_own, (1, 0, 3, 2))
    odd = (x == 1) | (x == 2)
    pivots = jnp.stack([choose(odd, coords_other, coords_own), choose(odd, coords_own, coords_other)])
    solves = solves[0:HALF]
    w = weights(pivots, coords)
    parts = [solves] + gather_x(solves, 2)

    swapped = odd.astype(jnp.int32)
    info = jnp.stack([row, swapped, *held(x, core, 2)]).astype(jnp.int32)
    scale_value = 1.0 / math.sqrt(SIDES * COLS)
    solved, table = final(
        info, adjoint_source, u_rows, forward_field, parts, field_steps[3:], w, pivots, coords, scale_value
    )

    table = table + lax.ppermute(table, "col", [(c, c ^ 1) for c in range(COLS)])
    others = [lax.ppermute(table, "col", [(c, (c + NC * k) % COLS) for c in range(COLS)]) for k in (1, 2, 3)]
    table = (table + others[1]) + (others[0] + others[2])
    slots = (pair_list[:, 0] * QB + pair_list[:, 1] - row * QB)[:, None, None]
    gradient = jnp.broadcast_to(table[:, 0, :][None], (pair_list.shape[0], 3, NB))
    for k in range(1, 2 * QB):
        gradient = jnp.where(slots == k, table[:, k, :][None], gradient)
    return solved, gradient


def solution(mesh):
    return jax.shard_map(
        on_device,
        mesh=mesh,
        in_specs=(P("col", "row"), P(None, None, "row"), P(), P("col", "row"), P(None, "row"), P("row", None)),
        out_specs=(P("col", "row"), P("row", None, None)),
        check_vma=False,
    )
```

```python
import math

import jax
import jax.numpy as jnp
from jax import lax
from jax.experimental import pallas as pl
from jax.experimental.pallas import tpu as pltpu
from jax.sharding import PartitionSpec as P

NZ, NX, NY, NC = 8, 4, 4, 2
ROWS, COLS = NZ * NX, NY * NC
NB, SIDES, WIDTH = 512, 256, 2048
QB = WIDTH // NB
HALF = SIDES // 2
CROWS = 16
FAR = 3
BF, F32 = jnp.bfloat16, jnp.float32
VMEM_LIMIT = 15 * 1024 * 1024


def node(z, x):
    return (z % NZ) * NX + x % NX


def shift(dz, dx, zs=range(NZ)):
    return [(node(z, x), node(z + dz, x + dx)) for z in zs for x in range(NX)]


def closed(pairs):
    out, back = dict(pairs), {d: s for s, d in pairs}
    for last in back:
        if last not in dict(pairs):
            first = last
            while first in back:
                first = back[first]
            out[last] = first
    return out


def send(value, pairs0, pairs1=None, idle="core"):
    maps = [closed(pairs0), closed(pairs0 if pairs1 is None else pairs1)]
    flip = 3 if idle == "y3" else 1
    out = {}
    for row in range(ROWS):
        free = [row not in maps[0], row not in maps[1]]
        for y in range(NY):
            for core in range(NC):
                me = row * COLS + y * NC + core
                if not free[core]:
                    out[me] = maps[core][row] * COLS + y * NC + core
                elif all(free) and idle == "core":
                    out[me] = row * COLS + y * NC + 1 - core
                else:
                    out[me] = row * COLS + (y ^ flip) * NC + core
    return lax.ppermute(value, ("row", "col"), sorted(out.items()))


def choose(condition, a, b):
    return lax.select(condition, a, b)


def swap_x(value, partner, zs=range(NZ)):
    return send(value, [(node(z, x), node(z, partner[x])) for z in zs for x in range(NX)])


def along_z(pairs):
    return [(node(a, x), node(b, x)) for a, b in pairs for x in range(NX)]


def spread_z(value, z):
    far = [send(value, along_z(((0, 3),))), send(value, along_z(((0, 5),)))]
    near = [send(value, along_z(((0, 1),))), send(value, along_z(((0, 7),)))]
    relays = choose(z == 3, far[0], choose(z == 5, far[1], value))
    near += [send(relays, along_z(((3, 4), (5, 6)))), send(relays, along_z(((3, 2),)))]
    held = choose(z == 1, near[0], choose(z == 7, near[1], relays))
    return choose((z == 4) | (z == 6), near[2], choose(z == 2, near[3], held))


def gather_x(value, twist):
    return [send(value, shift(0, j), shift(0, (j + twist - 1) % 3 + 1)) for j in (1, 2, 3)]


def moved(j, core, twist):
    return j if j == 0 else jnp.where(core == 0, j, (j + twist - 1) % 3 + 1)


def held(x, core, twist):
    return [(x - moved(j, core, twist)) % NX for j in range(NX)]


def dot(a, b):
    return jnp.dot(a, b, preferred_element_type=F32)


def in_hbm(array):
    return pltpu.with_memory_space_constraint(array, pltpu.HBM)


def halves_kernel(field, coords, first, second):
    for k, out in enumerate((first, second)):
        out[0:HALF, :] = field[k * HALF : (k + 1) * HALF, :]
        out[HALF:, :] = jnp.zeros((CROWS, NB), BF)
        out[HALF : HALF + 3, :] = coords[...]


def halves(field, coords):
    shape = (HALF + CROWS, NB)
    return pl.pallas_call(
        halves_kernel,
        grid=(1,),
        in_specs=[pl.BlockSpec((SIDES, NB), lambda i: (0, 0)), pl.BlockSpec((3, NB), lambda i: (0, 0))],
        out_specs=[pl.BlockSpec(shape, lambda i: (0, 0))] * 2,
        out_shape=[jax.ShapeDtypeStruct(shape, BF)] * 2,
    )(in_hbm(field), in_hbm(coords))


def exact_parts(value):
    high = value.astype(BF).astype(F32)
    middle = (value - high).astype(BF).astype(F32)
    return high, middle, value - high - middle


def lines_of(shape):
    return lax.broadcasted_iota(jnp.int32, shape, 0)


def final_kernel(
    info, source_ref, u_ref, field_ref, p0, p1, p2, p3, target_ref,
    solved_ref, grad_ref, s_ref, f_ref, both_ref, left_ref, right_ref, pivot_ref, near_ref, scale_value,
):
    q = pl.program_id(0)
    row = info[0]

    @pl.when(q == 0)
    def _():
        for j, ref in enumerate((p0, p1, p2, p3)):
            column = info[1 + j]
            a = (column ^ (column >> 1)) & 1
            start = pl.multiple_of((column >> 1) * HALF, HALF)
            s_ref[a, pl.ds(start, HALF), :] = ref[0:HALF, :]
            f_ref[a, pl.ds(start, HALF), :] = ref[HALF:SIDES, :]
            pivot_ref[a] = ref[SIDES:, :].astype(F32)
        for a in range(2):
            both_ref[:, a * NB : (a + 1) * NB] = s_ref[a]
            left_ref[a, :, 0:SIDES] = s_ref[a].T
            left_ref[a, :, SIDES:] = f_ref[a].T
            x = pivot_ref[a]
            line = lines_of(x.shape)
            near = jnp.where(line < 3, x, jnp.where(line < 9, 1.0, 0.0))
            for k, part in enumerate(exact_parts(jnp.sum(x * x, axis=0, keepdims=True))):
                near = jnp.where(line == 3 + k, part, near)
            near_ref[a] = near.T.astype(BF)

    solved_ref[...] = source_ref[...] - dot(both_ref[...], u_ref[...])

    @pl.when((q == 0) & (row < 2))
    def _():
        solved_ref[...] = s_ref[row].astype(F32)

    right_ref[0:SIDES, :] = field_ref[...]
    right_ref[SIDES:, :] = solved_ref[...].astype(BF)
    y = target_ref[...].astype(F32)
    line = lines_of(y.shape)
    far = jnp.where(line < 3, -2.0 * y, jnp.where(line < 6, 1.0, 0.0))
    for k, part in enumerate(exact_parts(jnp.sum(y * y, axis=0, keepdims=True) + 1.0)):
        far = jnp.where(line == 6 + k, part, far)
    far = far.astype(BF)
    target = jnp.where(line == 3, 1.0, y).astype(BF)
    for a in range(2):
        influence = dot(left_ref[a], right_ref[...])
        r = lax.rsqrt(dot(near_ref[a], far))
        weighted = (influence * (r * r * r)).astype(BF)
        sums = lax.dot_general(target, weighted, (((1,), (1,)), ((), ())), preferred_element_type=F32)
        source = pivot_ref[a]
        for c in range(3):
            grad_ref[c, pl.ds(a * QB + q, 1), :] = (
                sums[c : c + 1, :] - source[c : c + 1, :] * sums[3:4, :]
            ) * scale_value


def final(info, source, u_rows, field, parts, targets, scale_value):
    def whole(shape):
        return pl.BlockSpec(shape, lambda q, info: (0,) * len(shape))

    def body(info, *refs):
        final_kernel(info, *refs, scale_value)

    return pl.pallas_call(
        body,
        grid_spec=pltpu.PrefetchScalarGridSpec(
            num_scalar_prefetch=1,
            grid=(QB,),
            in_specs=[
                pl.BlockSpec((SIDES, NB), lambda q, info: (0, q)),
                pl.BlockSpec((2 * NB, NB), lambda q, info: (0, q)),
                pl.BlockSpec((SIDES, NB), lambda q, info: (0, q)),
                *[whole((SIDES + CROWS, NB))] * NX,
                pl.BlockSpec((CROWS, NB), lambda q, info: (0, q)),
            ],
            out_specs=[
                pl.BlockSpec((SIDES, NB), lambda q, info: (0, q)),
                whole((3, 2 * QB, NB)),
            ],
            scratch_shapes=[
                pltpu.VMEM((2, SIDES, NB), BF),
                pltpu.VMEM((2, SIDES, NB), BF),
                pltpu.VMEM((SIDES, 2 * NB), BF),
                pltpu.VMEM((2, NB, 2 * SIDES), BF),
                pltpu.VMEM((2 * SIDES, NB), BF),
                pltpu.VMEM((2, CROWS, NB), F32),
                pltpu.VMEM((2, NB, CROWS), BF),
            ],
        ),
        out_shape=[
            jax.ShapeDtypeStruct((SIDES, WIDTH), F32),
            jax.ShapeDtypeStruct((3, 2 * QB, NB), F32),
        ],
        cost_estimate=pl.CostEstimate(
            flops=4 * SIDES * NB * WIDTH + 8 * SIDES * NB * WIDTH, bytes_accessed=14 * 2**20, transcendentals=0
        ),
        compiler_params=pltpu.CompilerParams(vmem_limit_bytes=VMEM_LIMIT),
    )(info, in_hbm(source), in_hbm(u_rows.reshape(2 * NB, WIDTH)), in_hbm(field), *parts, targets)


def on_device(adjoint_source, u_rows, diag_inverse, forward_field, panel_coords, pair_list):
    row = lax.axis_index("row")
    z, x = row // NX, row % NX
    core = lax.axis_index("col") % NC
    head = adjoint_source[:, 0:NB]

    solve0 = dot(head.astype(BF), diag_inverse[0]).astype(BF)
    at_one = send(solve0, [(node(0, 0), node(0, 1))])

    later_field, later_coords, _ = lax.optimization_barrier((forward_field, panel_coords, solve0))
    first, second = halves(later_field, later_coords)
    fields = choose(x >= 2, swap_x(second, (3, 2, 1, 0), zs=(0,)), first)

    known0 = choose(x == 0, solve0, at_one)
    block1 = (head - dot(known0, u_rows[0, :, 0:NB])).astype(BF)
    solve1 = dot(block1, diag_inverse[1]).astype(BF)

    mine = choose(x == 0, solve0, solve1)
    solves = choose(x >= 2, swap_x(mine[HALF:], (3, 2, 1, 0), zs=(0,)), mine[0:HALF])
    value = jnp.concatenate([solves, fields], axis=0)
    value = spread_z(value, z)
    parts = [value] + gather_x(value, 2)

    coords = jnp.pad(panel_coords, ((0, CROWS - 3), (0, 0)))
    info = jnp.stack([row, *held(x, core, 2), ]).astype(jnp.int32)
    scale_value = 1.0 / math.sqrt(SIDES * COLS)
    solved, table = final(
        info, adjoint_source, u_rows, forward_field, parts, coords, scale_value
    )

    table = table + lax.ppermute(table, "col", [(c, c ^ 1) for c in range(COLS)])
    others = [lax.ppermute(table, "col", [(c, (c + NC * k) % COLS) for c in range(COLS)]) for k in (1, 2, 3)]
    table = (table + others[1]) + (others[0] + others[2])
    slots = (pair_list[:, 0] * QB + pair_list[:, 1] - row * QB)[:, None, None]
    gradient = jnp.broadcast_to(table[:, 0, :][None], (pair_list.shape[0], 3, NB))
    for k in range(1, 2 * QB):
        gradient = jnp.where(slots == k, table[:, k, :][None], gradient)
    return solved, gradient


def solution(mesh):
    return jax.shard_map(
        on_device,
        mesh=mesh,
        in_specs=(P("col", "row"), P(None, None, "row"), P(), P("col", "row"), P(None, "row"), P("row", None)),
        out_specs=(P("col", "row"), P("row", None, None)),
        check_vma=False,
    )
```

```python
import math

import jax
import jax.numpy as jnp
from jax import lax
from jax.experimental import pallas as pl
from jax.experimental.pallas import tpu as pltpu
from jax.sharding import PartitionSpec as P

NZ, NX, NY, NC = 8, 4, 4, 2
ROWS, COLS = NZ * NX, NY * NC
NB, SIDES, WIDTH = 512, 256, 2048
QB = WIDTH // NB
HALF = SIDES // 2
CROWS = 16
FAR = 3
BF, F32 = jnp.bfloat16, jnp.float32
UNROLL = 4
VMEM_LIMIT = 28 * 1024 * 1024


def node(z, x):
    return (z % NZ) * NX + x % NX


def shift(dz, dx, zs=range(NZ)):
    return [(node(z, x), node(z + dz, x + dx)) for z in zs for x in range(NX)]


def closed(pairs):
    out, back = dict(pairs), {d: s for s, d in pairs}
    for last in back:
        if last not in dict(pairs):
            first = last
            while first in back:
                first = back[first]
            out[last] = first
    return out


def send(value, pairs0, pairs1=None, idle="core"):
    maps = [closed(pairs0), closed(pairs0 if pairs1 is None else pairs1)]
    flip = 3 if idle == "y3" else 1
    out = {}
    for row in range(ROWS):
        free = [row not in maps[0], row not in maps[1]]
        for y in range(NY):
            for core in range(NC):
                me = row * COLS + y * NC + core
                if not free[core]:
                    out[me] = maps[core][row] * COLS + y * NC + core
                elif all(free) and idle == "core":
                    out[me] = row * COLS + y * NC + 1 - core
                else:
                    out[me] = row * COLS + (y ^ flip) * NC + core
    return lax.ppermute(value, ("row", "col"), sorted(out.items()))


def choose(condition, a, b):
    return lax.select(condition, a, b)


def swap_x(value, partner, zs=range(NZ)):
    return send(value, [(node(z, x), node(z, partner[x])) for z in zs for x in range(NX)])


def along_z(pairs):
    return [(node(a, x), node(b, x)) for a, b in pairs for x in range(NX)]


def spread_z(value, z):
    far = [send(value, along_z(((0, 3),))), send(value, along_z(((0, 5),)))]
    near = [send(value, along_z(((0, 1),))), send(value, along_z(((0, 7),)))]
    relays = choose(z == 3, far[0], choose(z == 5, far[1], value))
    near += [send(relays, along_z(((3, 4), (5, 6)))), send(relays, along_z(((3, 2),)))]
    held = choose(z == 1, near[0], choose(z == 7, near[1], relays))
    return choose((z == 4) | (z == 6), near[2], choose(z == 2, near[3], held))


def gather_x(value, twist):
    return [send(value, shift(0, j), shift(0, (j + twist - 1) % 3 + 1)) for j in (1, 2, 3)]


def moved(j, core, twist):
    return j if j == 0 else jnp.where(core == 0, j, (j + twist - 1) % 3 + 1)


def held(x, core, twist):
    return [(x - moved(j, core, twist)) % NX for j in range(NX)]


def dot(a, b):
    return jnp.dot(a, b, preferred_element_type=F32)


def in_hbm(array):
    return pltpu.with_memory_space_constraint(array, pltpu.HBM)


def halves_kernel(field, coords, first, second):
    for k, out in enumerate((first, second)):
        out[0:HALF, :] = field[k * HALF : (k + 1) * HALF, :]
        out[HALF:, :] = jnp.zeros((CROWS, NB), BF)
        out[HALF : HALF + 3, :] = coords[...]


def halves(field, coords):
    shape = (HALF + CROWS, NB)
    return pl.pallas_call(
        halves_kernel,
        grid=(1,),
        in_specs=[pl.BlockSpec((SIDES, NB), lambda i: (0, 0)), pl.BlockSpec((3, NB), lambda i: (0, 0))],
        out_specs=[pl.BlockSpec(shape, lambda i: (0, 0))] * 2,
        out_shape=[jax.ShapeDtypeStruct(shape, BF)] * 2,
    )(in_hbm(field), in_hbm(coords))


def exact_parts(value):
    high = value.astype(BF).astype(F32)
    middle = (value - high).astype(BF).astype(F32)
    return high, middle, value - high - middle


def lines_of(shape):
    return lax.broadcasted_iota(jnp.int32, shape, 0)


def final_kernel(
    info, source_ref, u_ref, field_ref, p0, p1, p2, p3, target_ref,
    solved_ref, grad_ref, s_ref, f_ref, both_ref, left_ref, right_ref, pivot_ref, near_ref, scale_value,
):
    step = pl.program_id(0)
    row = info[0]

    @pl.when(step == 0)
    def _():
        for j, ref in enumerate((p0, p1, p2, p3)):
            column = info[1 + j]
            a = (column ^ (column >> 1)) & 1
            start = pl.multiple_of((column >> 1) * HALF, HALF)
            s_ref[a, pl.ds(start, HALF), :] = ref[0:HALF, :]
            f_ref[a, pl.ds(start, HALF), :] = ref[HALF:SIDES, :]
            pivot_ref[a] = ref[SIDES:, :].astype(F32)
        for a in range(2):
            both_ref[:, a * NB : (a + 1) * NB] = s_ref[a]
            left_ref[a, :, 0:SIDES] = s_ref[a].T
            left_ref[a, :, SIDES:] = f_ref[a].T
            x = pivot_ref[a]
            line = lines_of(x.shape)
            near = jnp.where(line < 3, x, jnp.where(line < 9, 1.0, 0.0))
            for k, part in enumerate(exact_parts(jnp.sum(x * x, axis=0, keepdims=True))):
                near = jnp.where(line == 3 + k, part, near)
            near_ref[a] = near.T.astype(BF)

    for sub in range(UNROLL):
        here = slice(sub * NB, (sub + 1) * NB)
        block = pl.ds(pl.multiple_of(step * UNROLL * NB + sub * NB, NB), NB)
        solved_ref[:, here] = source_ref[:, block] - dot(both_ref[...], u_ref[:, block])

    @pl.when((step == 0) & (row < 2))
    def _():
        solved_ref[:, 0:NB] = s_ref[row].astype(F32)

    for sub in range(UNROLL):
        final_block(step * UNROLL + sub, sub, solved_ref, field_ref, target_ref, grad_ref, left_ref, right_ref.at[sub], pivot_ref, near_ref, scale_value)


def final_block(q, sub, solved_ref, field_ref, target_ref, grad_ref, left_ref, right_ref, pivot_ref, near_ref, scale_value):
    block = pl.ds(pl.multiple_of(q * NB, NB), NB)
    right_ref[0:SIDES, :] = field_ref[:, block]
    right_ref[SIDES:, :] = solved_ref[:, sub * NB : (sub + 1) * NB].astype(BF)
    y = target_ref[:, block].astype(F32)
    line = lines_of(y.shape)
    far = jnp.where(line < 3, -2.0 * y, jnp.where(line < 6, 1.0, 0.0))
    for k, part in enumerate(exact_parts(jnp.sum(y * y, axis=0, keepdims=True) + 1.0)):
        far = jnp.where(line == 6 + k, part, far)
    far = far.astype(BF)
    target = jnp.where(line == 3, 1.0, y).astype(BF)
    influence = dot(left_ref[...].reshape(2 * NB, 2 * SIDES), right_ref[...])
    r = lax.rsqrt(dot(near_ref[...].reshape(2 * NB, CROWS), far))
    weighted = (influence * (r * r * r)).astype(BF)
    sums = lax.dot_general(target, weighted, (((1,), (1,)), ((), ())), preferred_element_type=F32) * scale_value
    for a in range(2):
        here = sums[:, a * NB : (a + 1) * NB]
        source = pivot_ref[a]
        for c in range(3):
            grad_ref[c, pl.ds(a * QB + q, 1), :] = here[c : c + 1, :] - source[c : c + 1, :] * here[3:4, :]


def load_kernel(*refs):
    for k in range(len(refs) // 2):
        refs[len(refs) // 2 + k][...] = refs[k][...]


def load(*arrays):
    blocks = [pl.BlockSpec((array.shape[0], NB), lambda q: (0, q)) for array in arrays]
    return pl.pallas_call(
        load_kernel,
        grid=(QB,),
        in_specs=blocks,
        out_specs=blocks,
        out_shape=[jax.ShapeDtypeStruct(array.shape, array.dtype) for array in arrays],
        cost_estimate=pl.CostEstimate(flops=0, bytes_accessed=14 * 2**20, transcendentals=0),
        compiler_params=pltpu.CompilerParams(vmem_limit_bytes=VMEM_LIMIT),
    )(*[in_hbm(array) for array in arrays])


def final(info, source, u_rows, field, parts, targets, scale_value):
    def whole(shape):
        return pl.BlockSpec(shape, lambda q, info: (0,) * len(shape))

    def body(info, *refs):
        final_kernel(info, *refs, scale_value)

    return pl.pallas_call(
        body,
        grid_spec=pltpu.PrefetchScalarGridSpec(
            num_scalar_prefetch=1,
            grid=(QB // UNROLL,),
            in_specs=[pl.BlockSpec(memory_space=pltpu.VMEM)] * (4 + NX),
            out_specs=[
                pl.BlockSpec((SIDES, UNROLL * NB), lambda q, info: (0, q)),
                whole((3, 2 * QB, NB)),
            ],
            scratch_shapes=[
                pltpu.VMEM((2, SIDES, NB), BF),
                pltpu.VMEM((2, SIDES, NB), BF),
                pltpu.VMEM((SIDES, 2 * NB), BF),
                pltpu.VMEM((2, NB, 2 * SIDES), BF),
                pltpu.VMEM((UNROLL, 2 * SIDES, NB), BF),
                pltpu.VMEM((2, CROWS, NB), F32),
                pltpu.VMEM((2, NB, CROWS), BF),
            ],
        ),
        out_shape=[
            jax.ShapeDtypeStruct((SIDES, WIDTH), F32),
            jax.ShapeDtypeStruct((3, 2 * QB, NB), F32),
        ],
        cost_estimate=pl.CostEstimate(
            flops=4 * SIDES * NB * WIDTH + 8 * SIDES * NB * WIDTH, bytes_accessed=14 * 2**20, transcendentals=0
        ),
        compiler_params=pltpu.CompilerParams(vmem_limit_bytes=VMEM_LIMIT),
    )(info, source, u_rows, field, *parts, targets)


def on_device(adjoint_source, u_rows, diag_inverse, forward_field, panel_coords, pair_list):
    row = lax.axis_index("row")
    z, x = row // NX, row % NX
    core = lax.axis_index("col") % NC
    head = adjoint_source[:, 0:NB]

    solve0 = dot(head.astype(BF), diag_inverse[0]).astype(BF)
    at_one = send(solve0, [(node(0, 0), node(0, 1))])

    later_field, later_coords, _ = lax.optimization_barrier((forward_field, panel_coords, solve0))
    first, second = halves(later_field, later_coords)
    fields = choose(x >= 2, swap_x(second, (3, 2, 1, 0), zs=(0,)), first)

    own_head, own_factor, _ = lax.optimization_barrier((head, u_rows[0, :, 0:NB], solve0))
    known0 = choose(x == 0, solve0, at_one)
    block1 = (own_head - dot(known0, own_factor)).astype(BF)
    solve1 = dot(block1, diag_inverse[1]).astype(BF)

    mine = choose(x == 0, solve0, solve1)
    solves = choose(x >= 2, swap_x(mine[HALF:], (3, 2, 1, 0), zs=(0,)), mine[0:HALF])
    value = jnp.concatenate([solves, fields], axis=0)
    value = spread_z(value, z)
    source, factors, field, value = lax.optimization_barrier(
        (adjoint_source, u_rows.reshape(2 * NB, WIDTH), forward_field, value)
    )
    loaded = load(source, factors, field)
    parts = [value] + gather_x(value, 2)

    coords = jnp.pad(panel_coords, ((0, CROWS - 3), (0, 0)))
    info = jnp.stack([row, *held(x, core, 2), ]).astype(jnp.int32)
    scale_value = 1.0 / math.sqrt(SIDES * COLS)
    solved, table = final(
        info, *loaded, parts, coords, scale_value
    )

    table = table + lax.ppermute(table, "col", [(c, c ^ 1) for c in range(COLS)])
    across = lax.ppermute(table, "col", [(c, (c + NC * 2) % COLS) for c in range(COLS)])
    beside = lax.ppermute(table, "col", [(c, (c + (NC if c % NC == 0 else -NC)) % COLS) for c in range(COLS)])
    beside = beside + lax.ppermute(beside, "col", [(c, c ^ 1) for c in range(COLS)])
    table = (table + across) + beside
    slots = (pair_list[:, 0] * QB + pair_list[:, 1] - row * QB)[:, None, None]
    gradient = jnp.broadcast_to(table[:, 0, :][None], (pair_list.shape[0], 3, NB))
    for k in range(1, 2 * QB):
        gradient = jnp.where(slots == k, table[:, k, :][None], gradient)
    return solved, gradient


def solution(mesh):
    return jax.shard_map(
        on_device,
        mesh=mesh,
        in_specs=(P("col", "row"), P(None, None, "row"), P(), P("col", "row"), P(None, "row"), P("row", None)),
        out_specs=(P("col", "row"), P("row", None, None)),
        check_vma=False,
    )
```

```python
import math

import jax
import jax.numpy as jnp
from jax import lax
from jax.experimental import pallas as pl
from jax.experimental.pallas import tpu as pltpu
from jax.sharding import PartitionSpec as P

NZ, NX, NY, NC = 8, 4, 4, 2
ROWS, COLS = NZ * NX, NY * NC
NB, SIDES, WIDTH = 512, 256, 2048
QB = WIDTH // NB
HALF = SIDES // 2
CROWS = 16
FAR = 3
BF, F32 = jnp.bfloat16, jnp.float32
UNROLL = 4
VMEM_LIMIT = 28 * 1024 * 1024


def node(z, x):
    return (z % NZ) * NX + x % NX


def shift(dz, dx, zs=range(NZ)):
    return [(node(z, x), node(z + dz, x + dx)) for z in zs for x in range(NX)]


def closed(pairs):
    out, back = dict(pairs), {d: s for s, d in pairs}
    for last in back:
        if last not in dict(pairs):
            first = last
            while first in back:
                first = back[first]
            out[last] = first
    return out


def send(value, pairs0, pairs1=None, idle="core"):
    maps = [closed(pairs0), closed(pairs0 if pairs1 is None else pairs1)]
    flip = 3 if idle == "y3" else 1
    out = {}
    for row in range(ROWS):
        free = [row not in maps[0], row not in maps[1]]
        for y in range(NY):
            for core in range(NC):
                me = row * COLS + y * NC + core
                if not free[core]:
                    out[me] = maps[core][row] * COLS + y * NC + core
                elif all(free) and idle == "core":
                    out[me] = row * COLS + y * NC + 1 - core
                else:
                    out[me] = row * COLS + (y ^ flip) * NC + core
    return lax.ppermute(value, ("row", "col"), sorted(out.items()))


def choose(condition, a, b):
    return lax.select(condition, a, b)


def swap_x(value, partner, zs=range(NZ)):
    return send(value, [(node(z, x), node(z, partner[x])) for z in zs for x in range(NX)])


def along_z(pairs):
    return [(node(a, x), node(b, x)) for a, b in pairs for x in range(NX)]


def spread_z(value, z):
    far = [send(value, along_z(((0, 3),))), send(value, along_z(((0, 5),)))]
    near = [send(value, along_z(((0, 1),))), send(value, along_z(((0, 7),)))]
    relays = choose(z == 3, far[0], choose(z == 5, far[1], value))
    near += [send(relays, along_z(((3, 4), (5, 6)))), send(relays, along_z(((3, 2),)))]
    held = choose(z == 1, near[0], choose(z == 7, near[1], relays))
    return choose((z == 4) | (z == 6), near[2], choose(z == 2, near[3], held))


STEPS = ((1, 3), (3, 1), (2, 2))


def gather_x(value):
    return [send(value, shift(0, a), shift(0, b)) for a, b in STEPS]


def held(x, core):
    return [x] + [(x - jnp.where(core == 0, a, b)) % NX for a, b in STEPS]


def dot(a, b):
    return jnp.dot(a, b, preferred_element_type=F32)


def in_hbm(array):
    return pltpu.with_memory_space_constraint(array, pltpu.HBM)


def halves_kernel(field, coords, first, second):
    for k, out in enumerate((first, second)):
        out[0:HALF, :] = field[k * HALF : (k + 1) * HALF, :]
        out[HALF:, :] = jnp.zeros((CROWS, NB), BF)
        out[HALF : HALF + 3, :] = coords[...]


def halves(field, coords):
    shape = (HALF + CROWS, NB)
    return pl.pallas_call(
        halves_kernel,
        grid=(1,),
        in_specs=[pl.BlockSpec((SIDES, NB), lambda i: (0, 0)), pl.BlockSpec((3, NB), lambda i: (0, 0))],
        out_specs=[pl.BlockSpec(shape, lambda i: (0, 0))] * 2,
        out_shape=[jax.ShapeDtypeStruct(shape, BF)] * 2,
    )(in_hbm(field), in_hbm(coords))


def exact_parts(value):
    high = value.astype(BF).astype(F32)
    middle = (value - high).astype(BF).astype(F32)
    return high, middle, value - high - middle


def lines_of(shape):
    return lax.broadcasted_iota(jnp.int32, shape, 0)


def final_kernel(
    info, source_ref, u_ref, field_ref, p0, p1, p2, p3, target_ref,
    solved_ref, grad_ref, s_ref, f_ref, both_ref, left_ref, right_ref, pivot_ref, near_ref, scale_value,
):
    step = pl.program_id(0)
    row = info[0]

    @pl.when(step == 0)
    def _():
        for j, ref in enumerate((p0, p1, p2, p3)):
            column = info[1 + j]
            a = (column ^ (column >> 1)) & 1
            start = pl.multiple_of((column >> 1) * HALF, HALF)
            s_ref[a, pl.ds(start, HALF), :] = ref[0:HALF, :]
            f_ref[a, pl.ds(start, HALF), :] = ref[HALF:SIDES, :]
            pivot_ref[a] = ref[SIDES:, :].astype(F32)
        for a in range(2):
            both_ref[:, a * NB : (a + 1) * NB] = s_ref[a]
            left_ref[a, :, 0:SIDES] = s_ref[a].T
            left_ref[a, :, SIDES:] = f_ref[a].T
            x = pivot_ref[a]
            line = lines_of(x.shape)
            near = jnp.where(line < 3, x, jnp.where(line < 9, 1.0, 0.0))
            for k, part in enumerate(exact_parts(jnp.sum(x * x, axis=0, keepdims=True))):
                near = jnp.where(line == 3 + k, part, near)
            near_ref[a] = near.T.astype(BF)

    for sub in range(UNROLL):
        here = slice(sub * NB, (sub + 1) * NB)
        block = pl.ds(pl.multiple_of(step * UNROLL * NB + sub * NB, NB), NB)
        solved_ref[:, here] = source_ref[:, block] - dot(both_ref[...], u_ref[:, block])

    @pl.when((step == 0) & (row < 2))
    def _():
        solved_ref[:, 0:NB] = s_ref[row].astype(F32)

    for sub in range(UNROLL):
        final_block(step * UNROLL + sub, sub, solved_ref, field_ref, target_ref, grad_ref, left_ref, right_ref.at[sub], pivot_ref, near_ref, scale_value)


def final_block(q, sub, solved_ref, field_ref, target_ref, grad_ref, left_ref, right_ref, pivot_ref, near_ref, scale_value):
    block = pl.ds(pl.multiple_of(q * NB, NB), NB)
    right_ref[0:SIDES, :] = field_ref[:, block]
    right_ref[SIDES:, :] = solved_ref[:, sub * NB : (sub + 1) * NB].astype(BF)
    y = target_ref[:, block].astype(F32)
    line = lines_of(y.shape)
    far = jnp.where(line < 3, -2.0 * y, jnp.where(line < 6, 1.0, 0.0))
    for k, part in enumerate(exact_parts(jnp.sum(y * y, axis=0, keepdims=True) + 1.0)):
        far = jnp.where(line == 6 + k, part, far)
    far = far.astype(BF)
    target = jnp.where(line == 3, 1.0, y).astype(BF)
    influence = dot(left_ref[...].reshape(2 * NB, 2 * SIDES), right_ref[...])
    r = lax.rsqrt(dot(near_ref[...].reshape(2 * NB, CROWS), far))
    weighted = (influence * (r * r * r)).astype(BF)
    sums = lax.dot_general(target, weighted, (((1,), (1,)), ((), ())), preferred_element_type=F32) * scale_value
    for a in range(2):
        here = sums[:, a * NB : (a + 1) * NB]
        source = pivot_ref[a]
        for c in range(3):
            grad_ref[c, pl.ds(a * QB + q, 1), :] = here[c : c + 1, :] - source[c : c + 1, :] * here[3:4, :]


def load_kernel(*refs):
    for k in range(len(refs) // 2):
        refs[len(refs) // 2 + k][...] = refs[k][...]


def load(*arrays):
    blocks = [pl.BlockSpec((array.shape[0], NB), lambda q: (0, q)) for array in arrays]
    return pl.pallas_call(
        load_kernel,
        grid=(QB,),
        in_specs=blocks,
        out_specs=blocks,
        out_shape=[jax.ShapeDtypeStruct(array.shape, array.dtype) for array in arrays],
        cost_estimate=pl.CostEstimate(flops=0, bytes_accessed=14 * 2**20, transcendentals=0),
        compiler_params=pltpu.CompilerParams(vmem_limit_bytes=VMEM_LIMIT),
    )(*[in_hbm(array) for array in arrays])


def final(info, source, u_rows, field, parts, targets, scale_value):
    def whole(shape):
        return pl.BlockSpec(shape, lambda q, info: (0,) * len(shape))

    def body(info, *refs):
        final_kernel(info, *refs, scale_value)

    return pl.pallas_call(
        body,
        grid_spec=pltpu.PrefetchScalarGridSpec(
            num_scalar_prefetch=1,
            grid=(QB // UNROLL,),
            in_specs=[pl.BlockSpec(memory_space=pltpu.VMEM)] * (4 + NX),
            out_specs=[
                pl.BlockSpec((SIDES, UNROLL * NB), lambda q, info: (0, q)),
                whole((3, 2 * QB, NB)),
            ],
            scratch_shapes=[
                pltpu.VMEM((2, SIDES, NB), BF),
                pltpu.VMEM((2, SIDES, NB), BF),
                pltpu.VMEM((SIDES, 2 * NB), BF),
                pltpu.VMEM((2, NB, 2 * SIDES), BF),
                pltpu.VMEM((UNROLL, 2 * SIDES, NB), BF),
                pltpu.VMEM((2, CROWS, NB), F32),
                pltpu.VMEM((2, NB, CROWS), BF),
            ],
        ),
        out_shape=[
            jax.ShapeDtypeStruct((SIDES, WIDTH), F32),
            jax.ShapeDtypeStruct((3, 2 * QB, NB), F32),
        ],
        cost_estimate=pl.CostEstimate(
            flops=4 * SIDES * NB * WIDTH + 8 * SIDES * NB * WIDTH, bytes_accessed=14 * 2**20, transcendentals=0
        ),
        compiler_params=pltpu.CompilerParams(vmem_limit_bytes=VMEM_LIMIT),
    )(info, source, u_rows, field, *parts, targets)


def on_device(adjoint_source, u_rows, diag_inverse, forward_field, panel_coords, pair_list):
    row = lax.axis_index("row")
    z, x = row // NX, row % NX
    core = lax.axis_index("col") % NC
    head = adjoint_source[:, 0:NB]

    solve0 = dot(head.astype(BF), diag_inverse[0]).astype(BF)
    at_one = send(solve0, [(node(0, 0), node(0, 1))])

    later_field, later_coords, _ = lax.optimization_barrier((forward_field, panel_coords, solve0))
    first, second = halves(later_field, later_coords)
    fields = choose(x >= 2, swap_x(second, (3, 2, 1, 0), zs=(0,)), first)

    own_head, own_factor, _ = lax.optimization_barrier((head, u_rows[0, :, 0:NB], solve0))
    known0 = choose(x == 0, solve0, at_one)
    block1 = (own_head - dot(known0, own_factor)).astype(BF)
    solve1 = dot(block1, diag_inverse[1]).astype(BF)

    mine = choose(x == 0, solve0, solve1)
    solves = choose(x >= 2, swap_x(mine[HALF:], (3, 2, 1, 0), zs=(0,)), mine[0:HALF])
    value = jnp.concatenate([solves, fields], axis=0)
    value = spread_z(value, z)
    source, factors, field, value = lax.optimization_barrier(
        (adjoint_source, u_rows.reshape(2 * NB, WIDTH), forward_field, value)
    )
    loaded = load(source, factors, field)
    parts = [value] + gather_x(value)

    coords = jnp.pad(panel_coords, ((0, CROWS - 3), (0, 0)))
    info = jnp.stack([row, *held(x, core)]).astype(jnp.int32)
    scale_value = 1.0 / math.sqrt(SIDES * COLS)
    solved, table = final(
        info, *loaded, parts, coords, scale_value
    )

    table = table + lax.ppermute(table, "col", [(c, c ^ 1) for c in range(COLS)])
    across = lax.ppermute(table, "col", [(c, (c + NC * 2) % COLS) for c in range(COLS)])
    beside = lax.ppermute(table, "col", [(c, (c + (NC if c % NC == 0 else -NC)) % COLS) for c in range(COLS)])
    beside = beside + lax.ppermute(beside, "col", [(c, c ^ 1) for c in range(COLS)])
    table = (table + across) + beside
    slots = (pair_list[:, 0] * QB + pair_list[:, 1] - row * QB)[:, None, None]
    gradient = jnp.broadcast_to(table[:, 0, :][None], (pair_list.shape[0], 3, NB))
    for k in range(1, 2 * QB):
        gradient = jnp.where(slots == k, table[:, k, :][None], gradient)
    return solved, gradient


def solution(mesh):
    return jax.shard_map(
        on_device,
        mesh=mesh,
        in_specs=(P("col", "row"), P(None, None, "row"), P(), P("col", "row"), P(None, "row"), P("row", None)),
        out_specs=(P("col", "row"), P("row", None, None)),
        check_vma=False,
    )
```
